32 devices in a mesh: seq: 8 (over y, x, core), head: 4 (over z).
Axes of the slice: x: 2, y: 2, z: 4, core: 2. Of those that a mesh axis runs over, the one named last changes fastest.
Arguments:
- queries: bfloat16 [128, 8192], P('seq', 'head'), may hold values from -130 to 130
- grad_output: bfloat16 [128, 8192], P('seq', 'head'), may hold values from -384 to 384
- key_cache: bfloat16 [3072, 512], P('seq', 'head'), may hold values from -6 to 6
- saved_value_rows: bfloat16 [3072, 512], P('seq', 'head'), may hold values from -6 to 6
- lengths: int32 [8], P('seq'), may hold values from 1 to 384, 2304 in all
- span_index: int32 [1], replicated, may hold values from 4 to 17
- w_query: bfloat16 [4096, 8192], P('seq', 'head'), may hold values from -0.09375 to 0.09375
- key_projection_weight: bfloat16 [4096, 512], P(None, 'head'), may hold values from -0.09375 to 0.09375
- value_projection_weight: bfloat16 [4096, 512], P(None, 'head'), may hold values from -0.09375 to 0.09375
Outputs:
- saved_key_gradient: bfloat16 [3072, 512], P('seq', 'head')
- saved_value_gradient: bfloat16 [3072, 512], P('seq', 'head')
- cached_input_gradient: bfloat16 [3072, 4096], P('seq', 'head')
- grad_span_input: bfloat16 [128, 4096], P('head', 'seq')
The draws below stay inside these ranges and needn't reach their ends.
All inputs are finite; a program needn't handle non-finite values. No bound on the sum of `lengths` on one device may be relied on, other than what follows from the above.
Results may differ from the reference program's by a relative error of at most 0.02.
Values may be sent and summed in bfloat16 or wider, within the bound.
A program may use at most 64 MiB of HBM per device.

```python
import math
import jax
import jax.numpy as jnp
import numpy as np
from jax import lax

MODEL_WIDTH = 4096
QUERY_HEADS = 64
KEY_VALUE_HEADS = 4
HEAD_WIDTH = 128
QC = 128
OWNER_SLOTS = 384
TOTAL_SLOTS = 3072
LIVE = 2304
N_SEQ = 8


def cache_row_list(key):
    sampled_values = jnp.clip(jax.random.normal(jax.random.fold_in(key, 11), (TOTAL_SLOTS, KEY_VALUE_HEADS * HEAD_WIDTH), jnp.float32), -5.0, 5.0)
    return sampled_values


def draw_key_cache(key, part):
    return cache_row_list(key).astype(jnp.bfloat16)


def draw_queries(key, part):
    sampled_values = jnp.clip(jax.random.normal(jax.random.fold_in(key, 23), (QC, QUERY_HEADS * HEAD_WIDTH), jnp.float32), -5.0, 5.0)
    return sampled_values.astype(jnp.bfloat16)


def shard_levels(own_key, extent, pieces, smallest, top_value):
    def one(dim, parts):
        steps = jax.random.uniform(jax.random.fold_in(jax.random.fold_in(own_key, 6), dim), (parts,), jnp.float32, smallest / len(pieces), top_value / len(pieces))
        return jnp.repeat(jnp.exp(steps), extent[dim] // parts).reshape((-1,) + (1,) * (len(extent) - dim - 1))

    factor_of = one(*pieces[0])
    for cut in pieces[1:]:
        factor_of = factor_of * one(*cut)
    return factor_of


def profile(count, total, bound, skew):
    portions = [(1 << 20) // math.isqrt(rank ** skew) + 1 for rank in range(2, count + 1)]
    surplus, counts = total - bound - (count - 1), [1] * (count - 1)
    while surplus > 0:
        movable = [i for i in range(count - 1) if counts[i] < bound]
        pool, remaining = sum([portions[i] for i in movable]), surplus
        for i in movable:
            addition = min(bound - counts[i], max(1, remaining * portions[i] // pool), surplus)
            counts[i] = counts[i] + addition
            surplus = surplus - addition
    return np.array([bound] + counts)


def uneven(key, amount, total, reach, slope):
    if amount == 2:
        one = jax.random.randint(key, (), max(1, total - reach), min(reach, total - 1) + 1)
        return jnp.stack([one, total - one])
    tallies = jnp.asarray(profile(amount, total, reach, slope), jnp.int32)
    pairs = (amount - 1) // 2
    donor, sink = tallies[1:1 + 2 * pairs:2], tallies[2:2 + 2 * pairs:2]
    room = jnp.minimum(donor - 1, reach - sink)
    moved = jax.random.randint(jax.random.fold_in(key, 1), (pairs,), 0, 1 << 20) % (room + 1)
    tallies = tallies.at[1:1 + 2 * pairs:2].set(donor - moved).at[2:2 + 2 * pairs:2].set(sink + moved)
    return tallies[jax.random.permutation(jax.random.fold_in(key, 2), amount)]


def gaussian(stream_key, extent, scale, most, shards=(), kind=jnp.bfloat16):
    entries = scale * jax.random.normal(stream_key, extent, jnp.float32)
    if shards:
        entries = entries * shard_levels(stream_key, extent, shards, -0.22, 0.18)
    return jnp.clip(entries, -most, most).astype(kind)


def setup_inputs(seed: int = 0) -> dict:
    streams_of = jax.random.split(jax.random.key(seed), 10)
    queries = draw_queries(jax.random.fold_in(streams_of[9], 71), 0)
    grad_output = gaussian(streams_of[1], (QC, QUERY_HEADS * HEAD_WIDTH), 64.0, 384.0, ((0, 8), (1, 4)))
    key_cache = draw_key_cache(jax.random.fold_in(streams_of[9], 71), 0)
    saved_value_rows = gaussian(streams_of[3], (TOTAL_SLOTS, KEY_VALUE_HEADS * HEAD_WIDTH), 1.0, 6.0, ((0, 8), (1, 4)))
    lengths = uneven(streams_of[4], N_SEQ, LIVE, OWNER_SLOTS, 2).astype(jnp.int32)
    span_index = jax.random.randint(streams_of[5], (1,), LIVE // (4 * QC), LIVE // QC).astype(jnp.int32)
    w_query = gaussian(streams_of[6], (MODEL_WIDTH, QUERY_HEADS * HEAD_WIDTH), MODEL_WIDTH ** -0.5, 0.09375, ((0, 8), (1, 4)))
    key_projection_weight = gaussian(streams_of[7], (MODEL_WIDTH, KEY_VALUE_HEADS * HEAD_WIDTH), MODEL_WIDTH ** -0.5, 0.09375, ((1, 4),))
    value_projection_weight = gaussian(streams_of[8], (MODEL_WIDTH, KEY_VALUE_HEADS * HEAD_WIDTH), MODEL_WIDTH ** -0.5, 0.09375, ((1, 4),))
    return dict(queries=queries, grad_output=grad_output, key_cache=key_cache, saved_value_rows=saved_value_rows, lengths=lengths, span_index=span_index, w_query=w_query, key_projection_weight=key_projection_weight, value_projection_weight=value_projection_weight)


LOWEST_SCORE = -1.0e30


def head_backward(query_rows, output_grads, key_block, value_block, visible):
    score_scale = HEAD_WIDTH ** -0.5
    scores = jnp.dot(query_rows, key_block.T, preferred_element_type=jnp.float32) * score_scale
    row_peak = jnp.max(jnp.where(visible, scores, LOWEST_SCORE), axis=1, keepdims=True)
    exponentials = jnp.exp(jnp.where(visible, scores - row_peak, LOWEST_SCORE))
    weights = exponentials / jnp.sum(exponentials, axis=1, keepdims=True)
    weight_grads = jnp.dot(output_grads, value_block.T, preferred_element_type=jnp.float32)
    row_terms = jnp.sum(weights * weight_grads, axis=1, keepdims=True)
    score_grads = weights * (weight_grads - row_terms)
    weights_low = weights.astype(jnp.bfloat16)
    score_low = score_grads.astype(jnp.bfloat16)
    value_grads = jnp.dot(weights_low.T, output_grads, preferred_element_type=jnp.float32)
    key_grads = jnp.dot(score_low.T, query_rows, preferred_element_type=jnp.float32)
    query_grads = jnp.dot(score_low, key_block, preferred_element_type=jnp.float32) * score_scale
    return query_grads, key_grads, value_grads


def reference(queries, grad_output, key_cache, saved_value_rows, lengths, span_index, w_query, key_projection_weight, value_projection_weight):
    heads_per_group = QUERY_HEADS // KEY_VALUE_HEADS
    slot_count = key_cache.shape[0]
    offsets = (jnp.cumsum(lengths) - lengths).astype(jnp.int32)
    slot_ids = jnp.arange(slot_count, dtype=jnp.int32)
    owners = slot_ids // OWNER_SLOTS
    within = slot_ids - owners * OWNER_SLOTS
    positions = offsets[owners] + within
    query_positions = span_index[0] * QC + jnp.arange(QC, dtype=jnp.int32)
    visible = (within < lengths[owners])[None, :] & (positions[None, :] <= query_positions[:, None])
    query_parts = []
    key_parts = []
    value_parts = []
    for shared_key_head in range(KEY_VALUE_HEADS):
        first = shared_key_head * HEAD_WIDTH
        key_block = key_cache[:, first:first + HEAD_WIDTH]
        value_block = saved_value_rows[:, first:first + HEAD_WIDTH]
        start = shared_key_head * heads_per_group * HEAD_WIDTH
        query_heads = queries[:, start:start + heads_per_group * HEAD_WIDTH].reshape(QC, heads_per_group, HEAD_WIDTH).transpose(1, 0, 2)
        grad_heads = grad_output[:, start:start + heads_per_group * HEAD_WIDTH].reshape(QC, heads_per_group, HEAD_WIDTH).transpose(1, 0, 2)

        def one_head(carry, pair, key_block=key_block, value_block=value_block):
            query_grads, key_grads, value_grads = head_backward(pair[0], pair[1], key_block, value_block, visible)
            return (carry[0] + key_grads, carry[1] + value_grads), query_grads

        zero_sums = jnp.zeros((slot_count, HEAD_WIDTH), jnp.float32)
        (key_sum, value_sum), query_grads = lax.scan(one_head, (zero_sums, zero_sums), (query_heads, grad_heads))
        query_parts.append(query_grads.transpose(1, 0, 2).reshape(QC, heads_per_group * HEAD_WIDTH))
        key_parts.append(key_sum * (HEAD_WIDTH ** -0.5))
        value_parts.append(value_sum)
    saved_key_gradient = jnp.concatenate(key_parts, axis=1).astype(jnp.bfloat16)
    saved_value_gradient = jnp.concatenate(value_parts, axis=1).astype(jnp.bfloat16)
    query_low = jnp.concatenate(query_parts, axis=1).astype(jnp.bfloat16)
    grad_span_input = jnp.dot(query_low, w_query.T, preferred_element_type=jnp.float32).astype(jnp.bfloat16)
    joined_weights = []
    for shared_key_head in range(KEY_VALUE_HEADS):
        first = shared_key_head * HEAD_WIDTH
        joined_weights.append(jnp.concatenate([key_projection_weight[:, first:first + HEAD_WIDTH], value_projection_weight[:, first:first + HEAD_WIDTH]], axis=1))

    def owner_slot_block(pair):
        key_rows, value_rows = pair
        total = jnp.zeros((OWNER_SLOTS, MODEL_WIDTH), jnp.float32)
        for shared_key_head in range(KEY_VALUE_HEADS):
            first = shared_key_head * HEAD_WIDTH
            both = jnp.concatenate([key_rows[:, first:first + HEAD_WIDTH], value_rows[:, first:first + HEAD_WIDTH]], axis=1)
            partial_term = jnp.dot(both, joined_weights[shared_key_head].T, preferred_element_type=jnp.float32)
            rounded = lax.optimization_barrier(partial_term.astype(jnp.bfloat16))
            total = total + rounded.astype(jnp.float32)
        return total.astype(jnp.bfloat16)

    cached_input_gradient = lax.map(owner_slot_block, (saved_key_gradient.reshape(N_SEQ, OWNER_SLOTS, KEY_VALUE_HEADS * HEAD_WIDTH), saved_value_gradient.reshape(N_SEQ, OWNER_SLOTS, KEY_VALUE_HEADS * HEAD_WIDTH)))
    cached_input_gradient = cached_input_gradient.reshape(slot_count, MODEL_WIDTH)
    return (saved_key_gradient, saved_value_gradient, cached_input_gradient, grad_span_input)
```

```python
import functools
import math

import jax
import jax.numpy as jnp
from jax import lax
from jax.experimental import pallas as pl
from jax.experimental.pallas import tpu as pltpu
from jax.sharding import PartitionSpec as P

HEAD_WIDTH = 128


LOWEST_SCORE = -1e30
PEAK_FLOOR = -1e29
MESH = pl.DeviceIdType.MESH
NT = (((1,), (1,)), ((), ()))


def dot_nt(a, b):
    return lax.dot_general(a, b, NT, preferred_element_type=jnp.float32)


def dot_nn(a, b):
    return jnp.dot(a, b, preferred_element_type=jnp.float32)


def kernel(
    n, nh,
    q_in, g_in, k_ref, v_ref, len_ref, span_ref, wq_in, kw_in, vw_in,
    dk_out, dv_out, cached_out, span_out,
    q_all, g_all, kt, len_all, bias, e_buf, dp_buf, st_all, fac, rterm,
    dv_acc, dk_acc, dq_send, dq_recv, dq_all, wq, w_all, dkv_all, acc,
    span_acc, span_send, span_recv,
    loc_sem, q_sem, g_sem, a_sem, len_sem, st_sem, rs_sem, w_sem, wf_sem, z_sem, h_sem,
):
    me, hd = lax.axis_index("seq"), lax.axis_index("head")
    nchip = n // 2
    core, chip = lax.rem(me, 2), me // 2
    sib = me + 1 - 2 * core
    rows_own = q_in.shape[0]
    rows = rows_own * n
    slots = k_ref.shape[0]
    heads = q_in.shape[1] // HEAD_WIDTH
    hb = heads // n
    wid = hb * HEAD_WIDTH
    half_rows = heads // 2
    feats = kw_in.shape[0] // nh
    fh = feats // 2
    scale = HEAD_WIDTH ** (-0.5)

    def seq_peer(k):
        return lax.rem(me + k, n)

    def seq_from(k):
        return lax.rem(me + n - k, n)

    def head_peer(k):
        return lax.rem(hd + k, nh)

    def head_from(k):
        return lax.rem(hd + nh - k, nh)

    def remote(src, dst, ssem, rsem, s, h):
        return pltpu.make_async_remote_copy(
            src_ref=src, dst_ref=dst, send_sem=ssem, recv_sem=rsem,
            device_id=(s, h), device_id_type=MESH,
        )

    own_rows = pl.ds(pl.multiple_of(me * rows_own, rows_own), rows_own)
    own_feats = pl.ds(pl.multiple_of(hd * feats, feats), feats)
    local = [
        pltpu.make_async_copy(q_in, q_all.at[own_rows], loc_sem.at[0]),
        pltpu.make_async_copy(g_in, g_all.at[own_rows], loc_sem.at[1]),
        pltpu.make_async_copy(wq_in, wq, loc_sem.at[2]),
        pltpu.make_async_copy(kw_in.at[own_feats], w_all.at[2 * hd], loc_sem.at[3]),
        pltpu.make_async_copy(vw_in.at[own_feats], w_all.at[2 * hd + 1], loc_sem.at[4]),
    ]
    for c in local:
        c.start()
    len_all[me] = jnp.full((8, 128), len_ref[0], jnp.int32)

    barrier = pltpu.get_barrier_semaphore()
    for k in range(1, n):
        pl.semaphore_signal(barrier, inc=1, device_id=(seq_peer(k), hd), device_id_type=MESH)
    for k in range(1, nh):
        pl.semaphore_signal(barrier, inc=1, device_id=(me, head_peer(k)), device_id_type=MESH)
    pl.semaphore_wait(barrier, n - 1 + nh - 1)

    def chip_peer(k):
        return 2 * lax.rem(chip + k, nchip) + core

    def chip_from(k):
        return 2 * lax.rem(chip + nchip - k, nchip) + core

    def gather_copy(k, src, slot, sem):
        to = sib if k == 0 else chip_peer(k)
        return remote(src, slot(me), sem.at[0, k], sem.at[1, k], to, hd)

    def forward_copy(k, slot, sem):
        block = slot(chip_from(k))
        return remote(block, block, sem.at[2, k], sem.at[3, k], sib, hd)

    def gather_start(src, slot, sem):
        for k in range(nchip):
            gather_copy(k, src, slot, sem).start()

    def gather_relay(src, slot, sem):
        for k in range(1, nchip):
            gather_copy(k, src, slot, sem).wait_recv()
            forward_copy(k, slot, sem).start()

    def gather_finish(src, slot, sem):
        gather_copy(0, src, slot, sem).wait_recv()
        for k in range(1, nchip):
            forward_copy(k, slot, sem).wait_recv()

    def gather_drain(src, slot, sem):
        for k in range(nchip):
            gather_copy(k, src, slot, sem).wait_send()
        for k in range(1, nchip):
            forward_copy(k, slot, sem).wait_send()

    def row_slot(buf):
        return lambda s: buf.at[pl.ds(pl.multiple_of(s * rows_own, rows_own), rows_own)]

    q_args = (q_in, row_slot(q_all), q_sem)
    g_args = (g_in, row_slot(g_all), g_sem)
    a_args = (dq_all.at[me], lambda s: dq_all.at[s], a_sem)

    def len_copy(k):
        return remote(
            len_all.at[me], len_all.at[me], len_sem.at[0, k], len_sem.at[1, k], seq_peer(k), hd
        )

    gather_start(*q_args)
    for k in range(1, n):
        len_copy(k).start()
    gather_start(*g_args)

    core_feats = pl.ds(pl.multiple_of(core * fh, fh), fh)

    def weight_copy(k, which):
        to = head_peer(k)
        src = (kw_in, vw_in)[which].at[pl.ds(pl.multiple_of(to * feats + core * fh, fh), fh)]
        return remote(
            src, w_all.at[2 * hd + which, core_feats],
            w_sem.at[0, which, k], w_sem.at[1, which, k], me, to,
        )

    def weight_forward(k):
        block = w_all.at[pl.ds(2 * head_from(k), 2), core_feats]
        return remote(block, block, wf_sem.at[0, k], wf_sem.at[1, k], sib, hd)

    for k in range(1, nh):
        for which in range(2):
            weight_copy(k, which).start()

    kt[...] = k_ref[...].T
    gather_relay(*q_args)
    gather_relay(*g_args)

    for k in range(1, n):
        len_copy(k).wait_recv()
    offset = jnp.zeros((8, 128), jnp.int32)
    for t in range(n):
        offset = offset + len_all[t] * (t < me).astype(jnp.int32)
    within = lax.broadcasted_iota(jnp.int32, (slots, rows), 0)
    qpos = span_ref[0] * rows + lax.broadcasted_iota(jnp.int32, (slots, rows), 1)
    visible = (within < len_ref[0]) & (offset[0:1, 0:1] + within <= qpos)
    bias[...] = jnp.where(visible, 0.0, LOWEST_SCORE)

    local[0].wait()
    local[1].wait()
    gather_finish(*q_args)
    gather_finish(*g_args)

    def pair(buf, j):
        block = buf[:, pl.ds(pl.multiple_of(j * wid, wid), wid)]
        return jnp.concatenate(
            [block[:, i * HEAD_WIDTH : (i + 1) * HEAD_WIDTH] for i in range(hb)], axis=0
        )

    def st_copy(half, k):
        return remote(
            st_all.at[half, me], st_all.at[half, me],
            st_sem.at[0, half, k], st_sem.at[1, half, k], seq_peer(k), hd,
        )

    for half in range(2):

        def first(i, carry, half=half):
            place = lax.rem(chip + 1 + i, nchip)
            j = 2 * place + half
            s = dot_nt(k_ref[...], pair(q_all, j)) * (scale * math.log2(math.e))
            s = s + jnp.concatenate([bias[...]] * hb, axis=1)
            m = jnp.maximum(jnp.max(s, axis=0, keepdims=True), PEAK_FLOOR)
            e = jnp.exp2(s - m)
            dp = dot_nt(v_ref[...], pair(g_all, j))
            e_buf[j] = e
            dp_buf[j] = dp
            stats = (m, jnp.sum(e, axis=0, keepdims=True), jnp.sum(e * dp, axis=0, keepdims=True))
            for at, stat in enumerate(stats):
                for h in range(hb):
                    st_all[half, me, pl.ds(at * half_rows + place * hb + h, 1), :] = stat[
                        :, h * rows : (h + 1) * rows
                    ]
            return carry

        lax.fori_loop(0, nchip, first, 0)
        for k in range(1, n):
            st_copy(half, k).start()

    def rs_copy(k, to):
        return remote(dq_send.at[to], dq_recv.at[me], rs_sem.at[0, k], rs_sem.at[1, k], to, hd)

    dv_acc[...] = jnp.zeros_like(dv_acc)
    dk_acc[...] = jnp.zeros_like(dk_acc)
    for half in range(2):
        for k in range(1, n):
            st_copy(half, k).wait_recv()
        part = lambda t, at: st_all[half, t, at * half_rows : (at + 1) * half_rows, :]
        peak = part(0, 0)
        for t in range(1, n):
            peak = jnp.maximum(peak, part(t, 0))
        total = jnp.zeros_like(peak)
        numer = jnp.zeros_like(peak)
        for t in range(n):
            f = jnp.exp2(part(t, 0) - peak)
            total = total + part(t, 1) * f
            numer = numer + part(t, 2) * f
        fac[half] = jnp.exp2(part(me, 0) - peak) / total
        rterm[half] = numer / total

        def second(i, carry, half=half):
            place = lax.rem(chip + 1 + i, nchip)
            j = 2 * place + half
            line = lambda ref: jnp.concatenate(
                [ref[half, pl.ds(place * hb + h, 1), :] for h in range(hb)], axis=1
            )
            p = e_buf[j] * line(fac)
            ds = (p * (dp_buf[j] - line(rterm))).astype(jnp.bfloat16)
            dv_acc[...] += dot_nn(p.astype(jnp.bfloat16), pair(g_all, j))
            dq_send[j] = (dot_nn(kt[...], ds) * scale).astype(jnp.bfloat16)

            @pl.when(j != me)
            def _():
                rs_copy(lax.rem(j + n - me, n), j).start()

            dk_acc[...] += dot_nn(ds, pair(q_all, j))
            return carry

        lax.fori_loop(0, nchip, second, 0)

    dk_low = (dk_acc[...] * scale).astype(jnp.bfloat16)
    dv_low = dv_acc[...].astype(jnp.bfloat16)
    dkv_all[2 * hd] = dk_low
    dkv_all[2 * hd + 1] = dv_low

    def z_copy(k):
        block = dkv_all.at[pl.ds(2 * hd, 2)]
        return remote(block, block, z_sem.at[0, k], z_sem.at[1, k], me, head_peer(k))

    for k in range(1, nh):
        z_copy(k).start()
    dk_out[...] = dk_low
    dv_out[...] = dv_low

    total = dq_send[me].astype(jnp.float32)
    for k in range(1, n):
        rs_copy(k, seq_peer(k)).wait_recv()
        total = total + dq_recv[seq_from(k)].astype(jnp.float32)
    for h in range(hb):
        dq_all[me, :, h * HEAD_WIDTH : (h + 1) * HEAD_WIDTH] = (
            total[:, h * rows : (h + 1) * rows].T.astype(jnp.bfloat16)
        )
    gather_start(*a_args)

    for k in range(1, nh):
        weight_copy(k, 0).wait_recv()
        weight_copy(k, 1).wait_recv()
        weight_forward(k).start()

    local[3].wait()
    local[4].wait()
    tile = min(256, feats)

    def term(g, start, last):
        lhs = jnp.concatenate([dkv_all[2 * g], dkv_all[2 * g + 1]], axis=1)

        def one(i, carry):
            at = pl.ds(pl.multiple_of(i * tile, tile), tile)
            rhs = jnp.concatenate([w_all[2 * g, at, :], w_all[2 * g + 1, at, :]], axis=1)
            x = dot_nt(lhs, rhs)
            if not start:
                x = x + acc[:, at]
            if last:
                cached_out[:, at] = x.astype(cached_out.dtype)
            else:
                acc[:, at] = x
            return carry

        lax.fori_loop(0, feats // tile, one, 0)

    local[2].wait()
    gather_relay(*a_args)
    term(hd, True, nh == 1)

    def span_add(s):
        cols = pl.ds(pl.multiple_of(s * wid, wid), wid)
        return dot_nt(dq_all[s], wq[:, cols])

    span_acc[...] = span_add(me)
    for k in range(1, nchip):
        span_acc[...] += span_add(chip_from(k))
    gather_finish(*a_args)

    def other(i, carry):
        span_acc[...] += span_add(2 * i + 1 - core)
        return carry

    lax.fori_loop(0, nchip, other, 0)

    span_rows = rows // nh
    span_send[...] = span_acc[...].astype(jnp.bfloat16).reshape(span_send.shape)

    def h_copy(k):
        to = head_peer(k)
        return remote(span_send.at[to], span_recv.at[hd], h_sem.at[0, k], h_sem.at[1, k], me, to)

    for k in range(1, nh):
        h_copy(k).start()

    for k in range(1, nh):
        weight_forward(k).wait_recv()
        z_copy(k).wait_recv()
        term(head_from(k), False, k == nh - 1)

    own_span = pl.ds(pl.multiple_of(hd * span_rows, span_rows), span_rows)
    total = span_acc[own_span, :]
    for k in range(1, nh):
        h_copy(k).wait_recv()
        total = total + span_recv[head_from(k)].astype(jnp.float32)
    span_out[...] = total.astype(span_out.dtype)

    gather_drain(*q_args)
    gather_drain(*g_args)
    gather_drain(*a_args)
    for k in range(1, n):
        len_copy(k).wait_send()
        rs_copy(k, seq_peer(k)).wait_send()
        for half in range(2):
            st_copy(half, k).wait_send()
    for k in range(1, nh):
        weight_copy(k, 0).wait_send()
        weight_copy(k, 1).wait_send()
        weight_forward(k).wait_send()
        z_copy(k).wait_send()
        h_copy(k).wait_send()


def fused(
    n, nh, queries, grad_output, key_cache, saved_value_rows, lengths, span_index,
    w_query, key_projection_weight, value_projection_weight,
):
    rows_own, width = queries.shape
    rows, heads = rows_own * n, width // HEAD_WIDTH
    wid = width // n
    slots = key_cache.shape[0]
    feats = key_projection_weight.shape[0] // nh
    out_feats = w_query.shape[0]
    nchip = n // 2
    bf, f32 = jnp.bfloat16, jnp.float32
    vmem = pl.BlockSpec(memory_space=pltpu.VMEM)
    smem = pl.BlockSpec(memory_space=pltpu.SMEM)
    anym = pl.BlockSpec(memory_space=pl.ANY)
    dma = pltpu.SemaphoreType.DMA
    V = pltpu.VMEM
    hq = wid // HEAD_WIDTH * rows
    return pl.pallas_call(
        functools.partial(kernel, n, nh),
        out_shape=(
            jax.ShapeDtypeStruct((slots, HEAD_WIDTH), bf),
            jax.ShapeDtypeStruct((slots, HEAD_WIDTH), bf),
            jax.ShapeDtypeStruct((slots, feats), bf),
            jax.ShapeDtypeStruct((rows // nh, out_feats), bf),
        ),
        in_specs=[anym, anym, vmem, vmem, smem, smem, anym, anym, anym],
        out_specs=(vmem, vmem, vmem, vmem),
        scratch_shapes=[
            V((rows, width), bf),
            V((rows, width), bf),
            V((HEAD_WIDTH, slots), bf),
            V((n, 8, 128), jnp.int32),
            V((slots, rows), f32),
            V((n, slots, hq), f32),
            V((n, slots, hq), f32),
            V((2, n, 3 * heads // 2, rows), f32),
            V((2, heads // 2, rows), f32),
            V((2, heads // 2, rows), f32),
            V((slots, HEAD_WIDTH), f32),
            V((slots, HEAD_WIDTH), f32),
            V((n, HEAD_WIDTH, hq), bf),
            V((n, HEAD_WIDTH, hq), bf),
            V((n, rows, wid), bf),
            V((out_feats, width), bf),
            V((2 * nh, feats, HEAD_WIDTH), bf),
            V((2 * nh, slots, HEAD_WIDTH), bf),
            V((slots, feats), f32),
            V((rows, out_feats), f32),
            V((nh, rows // nh, out_feats), bf),
            V((nh, rows // nh, out_feats), bf),
            dma((5,)),
            dma((4, nchip)),
            dma((4, nchip)),
            dma((4, nchip)),
            dma((2, n)),
            dma((2, 2, n)),
            dma((2, n)),
            dma((2, 2, nh)),
            dma((2, nh)),
            dma((2, nh)),
            dma((2, nh)),
        ],
        compiler_params=pltpu.CompilerParams(
            collective_id=0, has_side_effects=True, vmem_limit_bytes=48 * 1024 * 1024
        ),
    )(
        queries, grad_output, key_cache, saved_value_rows, lengths, span_index,
        w_query, key_projection_weight, value_projection_weight,
    )


def prefix(part, axis, combine, identity):
    place = lax.axis_index(axis)
    gathered = lax.all_gather(part, axis)
    state = jnp.zeros_like(part) + jnp.asarray(identity, part.dtype)

    def one(lap, state):
        return combine(state, lax.dynamic_index_in_dim(gathered, lap, 0, False))

    return lax.fori_loop(0, place, one, state)


def merged(part, axis, combine):
    gathered = jax.tree.map(lambda a: lax.all_gather(a, axis), part)

    def take(source):
        return jax.tree.map(lambda a: lax.dynamic_index_in_dim(a, source, 0, False), gathered)

    return lax.fori_loop(
        1, lax.axis_size(axis), lambda source, state: combine(state, take(source)), take(0)
    )


def add_counts(earlier, later):
    return earlier + later


def pair_merge(first, second):
    joined_peak = jnp.maximum(first[0], second[0])
    first_factor = jnp.exp(first[0] - joined_peak)
    second_factor = jnp.exp(second[0] - joined_peak)
    return (joined_peak, first[1] * first_factor + second[1] * second_factor)


def local(
    queries,
    grad_output,
    key_cache,
    saved_value_rows,
    lengths,
    span_index,
    w_query,
    key_projection_weight,
    value_projection_weight,
):
    score_scale = HEAD_WIDTH ** (-0.5)
    offset = prefix(lengths, "seq", add_counts, jnp.zeros((1,), jnp.int32))
    query_all, grad_all = (
        lax.all_gather(queries, "seq", axis=0, tiled=True),
        lax.all_gather(grad_output, "seq", axis=0, tiled=True),
    )
    row_count = query_all.shape[0]
    block_size = key_cache.shape[0]
    heads_per_group = query_all.shape[1] // HEAD_WIDTH
    within = jnp.arange(block_size, dtype=jnp.int32)
    query_positions = span_index[0] * row_count + jnp.arange(row_count, dtype=jnp.int32)
    visible = (within < lengths[0])[None, :] & (
        (offset[0] + within)[None, :] <= query_positions[:, None]
    )
    visible = visible[None, :, :]
    query_heads = query_all.reshape(row_count, heads_per_group, HEAD_WIDTH)
    grad_heads = grad_all.reshape(row_count, heads_per_group, HEAD_WIDTH)
    scores = (
        jnp.einsum("ihd,pd->hip", query_heads, key_cache, preferred_element_type=jnp.float32)
        * score_scale
    )
    weight_grads = jnp.einsum(
        "ihd,pd->hip", grad_heads, saved_value_rows, preferred_element_type=jnp.float32
    )
    local_peak = jnp.max(jnp.where(visible, scores, LOWEST_SCORE), axis=2)
    local_exp = jnp.exp(jnp.where(visible, scores - local_peak[:, :, None], LOWEST_SCORE))
    local_total = jnp.sum(local_exp, axis=2)
    row_peak, row_total = merged((local_peak, local_total), "seq", pair_merge)
    weights = (
        jnp.exp(jnp.where(visible, scores - row_peak[:, :, None], LOWEST_SCORE))
        / row_total[:, :, None]
    )
    row_terms = lax.psum(jnp.sum(weights * weight_grads, axis=2), "seq")
    score_grads = weights * (weight_grads - row_terms[:, :, None])
    weights_low = weights.astype(jnp.bfloat16)
    score_low = score_grads.astype(jnp.bfloat16)
    value_grads = jnp.einsum(
        "hip,ihd->pd", weights_low, grad_heads, preferred_element_type=jnp.float32
    )
    key_grads = (
        jnp.einsum("hip,ihd->pd", score_low, query_heads, preferred_element_type=jnp.float32)
        * score_scale
    )
    query_part = (
        jnp.einsum("hip,pd->ihd", score_low, key_cache, preferred_element_type=jnp.float32)
        * score_scale
    )
    query_sum = lax.psum(query_part.reshape(row_count, heads_per_group * HEAD_WIDTH), "seq")
    query_low = query_sum.astype(jnp.bfloat16)
    span_part = jnp.dot(query_low, w_query.T, preferred_element_type=jnp.float32)
    grad_span_input = lax.psum_scatter(span_part, "head", scatter_dimension=0, tiled=True).astype(
        jnp.bfloat16
    )
    saved_key_gradient = key_grads.astype(jnp.bfloat16)
    saved_value_gradient = value_grads.astype(jnp.bfloat16)
    key_weights, value_weights = (
        lax.all_to_all(key_projection_weight, "head", split_axis=0, concat_axis=1, tiled=True),
        lax.all_to_all(value_projection_weight, "head", split_axis=0, concat_axis=1, tiled=True),
    )
    key_all, value_all = (
        lax.all_gather(saved_key_gradient, "head", axis=1, tiled=True),
        lax.all_gather(saved_value_gradient, "head", axis=1, tiled=True),
    )
    total = jnp.zeros((block_size, key_weights.shape[0]), jnp.float32)
    for member in range(lax.axis_size("head")):
        first = member * HEAD_WIDTH
        both = jnp.concatenate(
            [key_all[:, first : first + HEAD_WIDTH], value_all[:, first : first + HEAD_WIDTH]],
            axis=1,
        )
        joined = jnp.concatenate(
            [
                key_weights[:, first : first + HEAD_WIDTH],
                value_weights[:, first : first + HEAD_WIDTH],
            ],
            axis=1,
        )
        partial_term = jnp.dot(both, joined.T, preferred_element_type=jnp.float32)
        rounded = lax.optimization_barrier(partial_term.astype(jnp.bfloat16))
        total = total + rounded.astype(jnp.float32)
    cached_input_gradient = total.astype(jnp.bfloat16)
    return (saved_key_gradient, saved_value_gradient, cached_input_gradient, grad_span_input)


def solution(mesh):
    in_specs = (
        P("seq", "head"),
        P("seq", "head"),
        P("seq", "head"),
        P("seq", "head"),
        P("seq"),
        P(),
        P("seq", "head"),
        P(None, "head"),
        P(None, "head"),
    )
    out_specs = (P("seq", "head"), P("seq", "head"), P("seq", "head"), P("head", "seq"))
    n, nh = mesh.shape["seq"], mesh.shape["head"]

    def device(queries, *rest):
        rows_own, width = queries.shape
        rows, heads = rows_own * n, width // HEAD_WIDTH
        fits = (
            n % 2 == 0
            and rows_own % 16 == 0
            and rows % 128 == 0
            and heads % n == 0
            and (heads // 2) % 8 == 0
            and (rows // nh) % 16 == 0
        )
        if not fits:
            return local(queries, *rest)
        return fused(n, nh, queries, *rest)

    return jax.shard_map(device, mesh=mesh, in_specs=in_specs, out_specs=out_specs, check_vma=False)
```

```python
import functools
import math

import jax
import jax.numpy as jnp
from jax import lax
from jax.experimental import pallas as pl
from jax.experimental.pallas import tpu as pltpu
from jax.sharding import PartitionSpec as P

HEAD_WIDTH = 128


LOWEST_SCORE = -1e30
PEAK_FLOOR = -1e29
MESH = pl.DeviceIdType.MESH
NT = (((1,), (1,)), ((), ()))


def dot_nt(a, b):
    return lax.dot_general(a, b, NT, preferred_element_type=jnp.float32)


def dot_nn(a, b):
    return jnp.dot(a, b, preferred_element_type=jnp.float32)


def kernel(
    n, nh,
    q_in, g_in, k_in, v_in, len_ref, span_ref, wq_in, kw_in, vw_in,
    dk_out, dv_out, cached_out, span_out,
    q_all, g_all, k_ref, v_ref, kt, len_all, bias, e_buf, dp_buf, st_all, fac, rterm,
    dv_acc, dk_acc, dq_send, dq_recv, dq_all, wq, w_all, dkv_all, acc,
    span_acc, span_send, span_recv,
    loc_sem, q_sem, g_sem, a_sem, len_sem, st_sem, rs_sem, w_sem, wf_sem, z_sem, h_sem,
):
    me, hd = lax.axis_index("seq"), lax.axis_index("head")
    nchip = n // 2
    core, chip = lax.rem(me, 2), me // 2
    sib = me + 1 - 2 * core
    rows_own = q_in.shape[0]
    rows = rows_own * n
    slots = k_in.shape[0]
    heads = q_in.shape[1] // HEAD_WIDTH
    hb = heads // n
    wid = hb * HEAD_WIDTH
    half_rows = heads // 2
    feats = kw_in.shape[0] // nh
    fh = feats // 2
    scale = HEAD_WIDTH ** (-0.5)

    def seq_peer(k):
        return lax.rem(me + k, n)

    def seq_from(k):
        return lax.rem(me + n - k, n)

    def head_peer(k):
        return lax.rem(hd + k, nh)

    def head_from(k):
        return lax.rem(hd + nh - k, nh)

    def remote(src, dst, ssem, rsem, s, h):
        return pltpu.make_async_remote_copy(
            src_ref=src, dst_ref=dst, send_sem=ssem, recv_sem=rsem,
            device_id=(s, h), device_id_type=MESH,
        )

    own_rows = pl.ds(pl.multiple_of(me * rows_own, rows_own), rows_own)
    own_feats = pl.ds(pl.multiple_of(hd * feats, feats), feats)
    local = [
        pltpu.make_async_copy(q_in, q_all.at[own_rows], loc_sem.at[0]),
        pltpu.make_async_copy(g_in, g_all.at[own_rows], loc_sem.at[1]),
        pltpu.make_async_copy(wq_in, wq, loc_sem.at[2]),
        pltpu.make_async_copy(kw_in.at[own_feats], w_all.at[2 * hd], loc_sem.at[3]),
        pltpu.make_async_copy(vw_in.at[own_feats], w_all.at[2 * hd + 1], loc_sem.at[4]),
        pltpu.make_async_copy(k_in, k_ref, loc_sem.at[5]),
        pltpu.make_async_copy(v_in, v_ref, loc_sem.at[6]),
    ]
    for c in local:
        c.start()
    len_all[me] = jnp.full((8, 128), len_ref[0], jnp.int32)

    barrier = pltpu.get_barrier_semaphore()
    for k in range(1, n):
        pl.semaphore_signal(barrier, inc=1, device_id=(seq_peer(k), hd), device_id_type=MESH)
    for k in range(1, nh):
        pl.semaphore_signal(barrier, inc=1, device_id=(me, head_peer(k)), device_id_type=MESH)
    pl.semaphore_wait(barrier, n - 1 + nh - 1)

    def chip_peer(k):
        return 2 * lax.rem(chip + k, nchip) + core

    def chip_from(k):
        return 2 * lax.rem(chip + nchip - k, nchip) + core

    def gather_copy(k, src, slot, sem):
        to = sib if k == 0 else chip_peer(k)
        return remote(src, slot(me), sem.at[0, k], sem.at[1, k], to, hd)

    def forward_copy(k, slot, sem):
        block = slot(chip_from(k))
        return remote(block, block, sem.at[2, k], sem.at[3, k], sib, hd)

    def gather_start(src, slot, sem):
        for k in range(nchip):
            gather_copy(k, src, slot, sem).start()

    def gather_relay(src, slot, sem):
        for k in range(1, nchip):
            gather_copy(k, src, slot, sem).wait_recv()
            forward_copy(k, slot, sem).start()

    def gather_finish(src, slot, sem):
        gather_copy(0, src, slot, sem).wait_recv()
        for k in range(1, nchip):
            forward_copy(k, slot, sem).wait_recv()

    def gather_drain(src, slot, sem):
        for k in range(nchip):
            gather_copy(k, src, slot, sem).wait_send()
        for k in range(1, nchip):
            forward_copy(k, slot, sem).wait_send()

    def row_slot(buf):
        return lambda s: buf.at[pl.ds(pl.multiple_of(s * rows_own, rows_own), rows_own)]

    q_args = (q_in, row_slot(q_all), q_sem)
    g_args = (g_in, row_slot(g_all), g_sem)
    a_args = (dq_all.at[me], lambda s: dq_all.at[s], a_sem)

    def len_copy(k):
        return remote(
            len_all.at[me], len_all.at[me], len_sem.at[0, k], len_sem.at[1, k], seq_peer(k), hd
        )

    gather_start(*q_args)
    for k in range(1, n):
        len_copy(k).start()
    gather_start(*g_args)

    core_feats = pl.ds(pl.multiple_of(core * fh, fh), fh)

    def weight_copy(k, which):
        to = head_peer(k)
        src = (kw_in, vw_in)[which].at[pl.ds(pl.multiple_of(to * feats + core * fh, fh), fh)]
        return remote(
            src, w_all.at[2 * hd + which, core_feats],
            w_sem.at[0, which, k], w_sem.at[1, which, k], me, to,
        )

    def weight_forward(k):
        block = w_all.at[pl.ds(2 * head_from(k), 2), core_feats]
        return remote(block, block, wf_sem.at[0, k], wf_sem.at[1, k], sib, hd)

    for k in range(1, nh):
        for which in range(2):
            weight_copy(k, which).start()

    local[5].wait()
    kt[...] = k_ref[...].T
    local[6].wait()
    gather_relay(*q_args)
    gather_relay(*g_args)

    for k in range(1, n):
        len_copy(k).wait_recv()
    offset = jnp.zeros((8, 128), jnp.int32)
    for t in range(n):
        offset = offset + len_all[t] * (t < me).astype(jnp.int32)
    within = lax.broadcasted_iota(jnp.int32, (slots, rows), 0)
    qpos = span_ref[0] * rows + lax.broadcasted_iota(jnp.int32, (slots, rows), 1)
    visible = (within < len_ref[0]) & (offset[0:1, 0:1] + within <= qpos)
    bias[...] = jnp.where(visible, 0.0, LOWEST_SCORE)

    local[0].wait()
    local[1].wait()
    gather_finish(*q_args)
    gather_finish(*g_args)

    def pair(buf, j):
        block = buf[:, pl.ds(pl.multiple_of(j * wid, wid), wid)]
        return jnp.concatenate(
            [block[:, i * HEAD_WIDTH : (i + 1) * HEAD_WIDTH] for i in range(hb)], axis=0
        )

    def st_copy(half, k):
        return remote(
            st_all.at[half, me], st_all.at[half, me],
            st_sem.at[0, half, k], st_sem.at[1, half, k], seq_peer(k), hd,
        )

    for half in range(2):

        def first(i, carry, half=half):
            place = lax.rem(chip + 1 + i, nchip)
            j = 2 * place + half
            s = dot_nt(k_ref[...], pair(q_all, j)) * (scale * math.log2(math.e))
            s = s + jnp.concatenate([bias[...]] * hb, axis=1)
            m = jnp.maximum(jnp.max(s, axis=0, keepdims=True), PEAK_FLOOR)
            e = jnp.exp2(s - m)
            dp = dot_nt(v_ref[...], pair(g_all, j))
            e_buf[j] = e
            dp_buf[j] = dp
            stats = (m, jnp.sum(e, axis=0, keepdims=True), jnp.sum(e * dp, axis=0, keepdims=True))
            for at, stat in enumerate(stats):
                for h in range(hb):
                    st_all[half, me, pl.ds(at * half_rows + place * hb + h, 1), :] = stat[
                        :, h * rows : (h + 1) * rows
                    ]
            return carry

        lax.fori_loop(0, nchip, first, 0)
        for k in range(1, n):
            st_copy(half, k).start()

    def rs_copy(k, to):
        return remote(dq_send.at[to], dq_recv.at[me], rs_sem.at[0, k], rs_sem.at[1, k], to, hd)

    dv_acc[...] = jnp.zeros_like(dv_acc)
    dk_acc[...] = jnp.zeros_like(dk_acc)
    for half in range(2):
        for k in range(1, n):
            st_copy(half, k).wait_recv()
        part = lambda t, at: st_all[half, t, at * half_rows : (at + 1) * half_rows, :]
        peak = part(0, 0)
        for t in range(1, n):
            peak = jnp.maximum(peak, part(t, 0))
        total = jnp.zeros_like(peak)
        numer = jnp.zeros_like(peak)
        for t in range(n):
            f = jnp.exp2(part(t, 0) - peak)
            total = total + part(t, 1) * f
            numer = numer + part(t, 2) * f
        fac[half] = jnp.exp2(part(me, 0) - peak) / total
        rterm[half] = numer / total

        def second(i, carry, half=half):
            place = lax.rem(chip + 1 + i, nchip)
            j = 2 * place + half
            line = lambda ref: jnp.concatenate(
                [ref[half, pl.ds(place * hb + h, 1), :] for h in range(hb)], axis=1
            )
            p = e_buf[j] * line(fac)
            ds = (p * (dp_buf[j] - line(rterm))).astype(jnp.bfloat16)
            dv_acc[...] += dot_nn(p.astype(jnp.bfloat16), pair(g_all, j))
            dq_send[j] = (dot_nn(kt[...], ds) * scale).astype(jnp.bfloat16)

            @pl.when(j != me)
            def _():
                rs_copy(lax.rem(j + n - me, n), j).start()

            dk_acc[...] += dot_nn(ds, pair(q_all, j))
            return carry

        lax.fori_loop(0, nchip, second, 0)

    dk_low = (dk_acc[...] * scale).astype(jnp.bfloat16)
    dv_low = dv_acc[...].astype(jnp.bfloat16)
    dkv_all[2 * hd] = dk_low
    dkv_all[2 * hd + 1] = dv_low

    def z_send(way, d):
        src = hd - (d - 1) if way == 0 else hd + (d - 1)
        to = hd + 1 if way == 0 else hd - 1
        block = dkv_all.at[pl.ds(2 * src, 2)]
        ok = (src >= 0) & (src < nh) & (to >= 0) & (to < nh)
        return ok, remote(block, block, z_sem.at[0, way, d], z_sem.at[1, way, d], me, to)

    def z_recv(way, d):
        src = hd - d if way == 0 else hd + d
        block = dkv_all.at[pl.ds(2 * src, 2)]
        ok = (src >= 0) & (src < nh)
        return ok, src, remote(
            block, block, z_sem.at[0, way, d], z_sem.at[1, way, d], me, head_peer(1)
        )

    def z_start(d):
        for way in range(2):
            ok, c = z_send(way, d)
            pl.when(ok)(c.start)

    def z_hop(d):
        for way in range(2):
            ok, _, c = z_recv(way, d - 1)
            pl.when(ok)(c.wait_recv)
        z_start(d)

    z_start(1)
    dk_out[...] = dk_low
    dv_out[...] = dv_low

    total = dq_send[me].astype(jnp.float32)
    for k in range(1, n):
        rs_copy(k, seq_peer(k)).wait_recv()
        total = total + dq_recv[seq_from(k)].astype(jnp.float32)
    for h in range(hb):
        dq_all[me, :, h * HEAD_WIDTH : (h + 1) * HEAD_WIDTH] = (
            total[:, h * rows : (h + 1) * rows].T.astype(jnp.bfloat16)
        )
    gather_start(*a_args)

    z_hop(2)
    for k in range(1, nh):
        weight_copy(k, 0).wait_recv()
        weight_copy(k, 1).wait_recv()
        weight_forward(k).start()

    local[3].wait()
    local[4].wait()
    tile = min(256, feats)

    def term(g, start):
        lhs = jnp.concatenate([dkv_all[2 * g], dkv_all[2 * g + 1]], axis=1)

        def one(i, carry):
            at = pl.ds(pl.multiple_of(i * tile, tile), tile)
            rhs = jnp.concatenate([w_all[2 * g, at, :], w_all[2 * g + 1, at, :]], axis=1)
            x = dot_nt(lhs, rhs)
            acc[:, at] = x if start else x + acc[:, at]
            return carry

        lax.fori_loop(0, feats // tile, one, 0)

    local[2].wait()
    gather_relay(*a_args)
    term(hd, True)

    def span_add(s):
        cols = pl.ds(pl.multiple_of(s * wid, wid), wid)
        return dot_nt(dq_all[s], wq[:, cols])

    span_acc[...] = span_add(me)
    for k in range(1, nchip):
        span_acc[...] += span_add(chip_from(k))
    gather_finish(*a_args)

    def other(i, carry):
        span_acc[...] += span_add(2 * i + 1 - core)
        return carry

    lax.fori_loop(0, nchip, other, 0)

    span_rows = rows // nh
    span_send[...] = span_acc[...].astype(jnp.bfloat16).reshape(span_send.shape)

    def h_copy(k):
        to = head_peer(k)
        return remote(span_send.at[to], span_recv.at[hd], h_sem.at[0, k], h_sem.at[1, k], me, to)

    for k in range(1, nh):
        h_copy(k).start()

    for d in range(3, nh):
        z_hop(d)
    for k in range(1, nh):
        weight_forward(k).wait_recv()
    for d in range(1, nh):
        for way in range(2):
            ok, src, c = z_recv(way, d)

            @pl.when(ok)
            def _(src=src, c=c, d=d, way=way):
                if d == nh - 1:
                    c.wait_recv()
                term(src, False)

    cached_out[...] = acc[...].astype(cached_out.dtype)

    own_span = pl.ds(pl.multiple_of(hd * span_rows, span_rows), span_rows)
    total = span_acc[own_span, :]
    for k in range(1, nh):
        h_copy(k).wait_recv()
        total = total + span_recv[head_from(k)].astype(jnp.float32)
    span_out[...] = total.astype(span_out.dtype)

    gather_drain(*q_args)
    gather_drain(*g_args)
    gather_drain(*a_args)
    for k in range(1, n):
        len_copy(k).wait_send()
        rs_copy(k, seq_peer(k)).wait_send()
        for half in range(2):
            st_copy(half, k).wait_send()
    for k in range(1, nh):
        weight_copy(k, 0).wait_send()
        weight_copy(k, 1).wait_send()
        weight_forward(k).wait_send()
        for way in range(2):
            ok, c = z_send(way, k)
            pl.when(ok)(c.wait_send)
        h_copy(k).wait_send()


def fused(
    n, nh, queries, grad_output, key_cache, saved_value_rows, lengths, span_index,
    w_query, key_projection_weight, value_projection_weight,
):
    rows_own, width = queries.shape
    rows, heads = rows_own * n, width // HEAD_WIDTH
    wid = width // n
    slots = key_cache.shape[0]
    feats = key_projection_weight.shape[0] // nh
    out_feats = w_query.shape[0]
    nchip = n // 2
    bf, f32 = jnp.bfloat16, jnp.float32
    vmem = pl.BlockSpec(memory_space=pltpu.VMEM)
    smem = pl.BlockSpec(memory_space=pltpu.SMEM)
    hbm = pl.BlockSpec(memory_space=pltpu.HBM)
    dma = pltpu.SemaphoreType.DMA
    V = pltpu.VMEM
    hq = wid // HEAD_WIDTH * rows
    results = pl.pallas_call(
        functools.partial(kernel, n, nh),
        out_shape=(
            jax.ShapeDtypeStruct((slots, HEAD_WIDTH), bf),
            jax.ShapeDtypeStruct((slots, HEAD_WIDTH), bf),
            jax.ShapeDtypeStruct((slots, feats), bf),
            jax.ShapeDtypeStruct((rows // nh, out_feats), bf),
        ),
        in_specs=[hbm, hbm, hbm, hbm, smem, smem, hbm, hbm, hbm],
        out_specs=(vmem, vmem, vmem, vmem),
        scratch_shapes=[
            V((rows, width), bf),
            V((rows, width), bf),
            V((slots, HEAD_WIDTH), bf),
            V((slots, HEAD_WIDTH), bf),
            V((HEAD_WIDTH, slots), bf),
            V((n, 8, 128), jnp.int32),
            V((slots, rows), f32),
            V((n, slots, hq), f32),
            V((n, slots, hq), f32),
            V((2, n, 3 * heads // 2, rows), f32),
            V((2, heads // 2, rows), f32),
            V((2, heads // 2, rows), f32),
            V((slots, HEAD_WIDTH), f32),
            V((slots, HEAD_WIDTH), f32),
            V((n, HEAD_WIDTH, hq), bf),
            V((n, HEAD_WIDTH, hq), bf),
            V((n, rows, wid), bf),
            V((out_feats, width), bf),
            V((2 * nh, feats, HEAD_WIDTH), bf),
            V((2 * nh, slots, HEAD_WIDTH), bf),
            V((slots, feats), f32),
            V((rows, out_feats), f32),
            V((nh, rows // nh, out_feats), bf),
            V((nh, rows // nh, out_feats), bf),
            dma((7,)),
            dma((4, nchip)),
            dma((4, nchip)),
            dma((4, nchip)),
            dma((2, n)),
            dma((2, 2, n)),
            dma((2, n)),
            dma((2, 2, nh)),
            dma((2, nh)),
            dma((2, 2, nh)),
            dma((2, nh)),
        ],
        compiler_params=pltpu.CompilerParams(
            collective_id=0, has_side_effects=True, vmem_limit_bytes=63 * 1024 * 1024
        ),
    )(
        queries, grad_output, key_cache, saved_value_rows, lengths, span_index,
        w_query, key_projection_weight, value_projection_weight,
    )
    count = len(results)
    return pl.pallas_call(
        functools.partial(write_out, count),
        out_shape=tuple(jax.ShapeDtypeStruct(r.shape, r.dtype) for r in results),
        in_specs=[vmem] * count,
        out_specs=(hbm,) * count,
        scratch_shapes=[dma((count,))],
    )(*results)


def write_out(count, *refs):
    sem = refs[-1]
    copies = [
        pltpu.make_async_copy(refs[i], refs[count + i], sem.at[i]) for i in range(count)
    ]
    for c in copies:
        c.start()
    for c in copies:
        c.wait()


def prefix(part, axis, combine, identity):
    place = lax.axis_index(axis)
    gathered = lax.all_gather(part, axis)
    state = jnp.zeros_like(part) + jnp.asarray(identity, part.dtype)

    def one(lap, state):
        return combine(state, lax.dynamic_index_in_dim(gathered, lap, 0, False))

    return lax.fori_loop(0, place, one, state)


def merged(part, axis, combine):
    gathered = jax.tree.map(lambda a: lax.all_gather(a, axis), part)

    def take(source):
        return jax.tree.map(lambda a: lax.dynamic_index_in_dim(a, source, 0, False), gathered)

    return lax.fori_loop(
        1, lax.axis_size(axis), lambda source, state: combine(state, take(source)), take(0)
    )


def add_counts(earlier, later):
    return earlier + later


def pair_merge(first, second):
    joined_peak = jnp.maximum(first[0], second[0])
    first_factor = jnp.exp(first[0] - joined_peak)
    second_factor = jnp.exp(second[0] - joined_peak)
    return (joined_peak, first[1] * first_factor + second[1] * second_factor)


def local(
    queries,
    grad_output,
    key_cache,
    saved_value_rows,
    lengths,
    span_index,
    w_query,
    key_projection_weight,
    value_projection_weight,
):
    score_scale = HEAD_WIDTH ** (-0.5)
    offset = prefix(lengths, "seq", add_counts, jnp.zeros((1,), jnp.int32))
    query_all, grad_all = (
        lax.all_gather(queries, "seq", axis=0, tiled=True),
        lax.all_gather(grad_output, "seq", axis=0, tiled=True),
    )
    row_count = query_all.shape[0]
    block_size = key_cache.shape[0]
    heads_per_group = query_all.shape[1] // HEAD_WIDTH
    within = jnp.arange(block_size, dtype=jnp.int32)
    query_positions = span_index[0] * row_count + jnp.arange(row_count, dtype=jnp.int32)
    visible = (within < lengths[0])[None, :] & (
        (offset[0] + within)[None, :] <= query_positions[:, None]
    )
    visible = visible[None, :, :]
    query_heads = query_all.reshape(row_count, heads_per_group, HEAD_WIDTH)
    grad_heads = grad_all.reshape(row_count, heads_per_group, HEAD_WIDTH)
    scores = (
        jnp.einsum("ihd,pd->hip", query_heads, key_cache, preferred_element_type=jnp.float32)
        * score_scale
    )
    weight_grads = jnp.einsum(
        "ihd,pd->hip", grad_heads, saved_value_rows, preferred_element_type=jnp.float32
    )
    local_peak = jnp.max(jnp.where(visible, scores, LOWEST_SCORE), axis=2)
    local_exp = jnp.exp(jnp.where(visible, scores - local_peak[:, :, None], LOWEST_SCORE))
    local_total = jnp.sum(local_exp, axis=2)
    row_peak, row_total = merged((local_peak, local_total), "seq", pair_merge)
    weights = (
        jnp.exp(jnp.where(visible, scores - row_peak[:, :, None], LOWEST_SCORE))
        / row_total[:, :, None]
    )
    row_terms = lax.psum(jnp.sum(weights * weight_grads, axis=2), "seq")
    score_grads = weights * (weight_grads - row_terms[:, :, None])
    weights_low = weights.astype(jnp.bfloat16)
    score_low = score_grads.astype(jnp.bfloat16)
    value_grads = jnp.einsum(
        "hip,ihd->pd", weights_low, grad_heads, preferred_element_type=jnp.float32
    )
    key_grads = (
        jnp.einsum("hip,ihd->pd", score_low, query_heads, preferred_element_type=jnp.float32)
        * score_scale
    )
    query_part = (
        jnp.einsum("hip,pd->ihd", score_low, key_cache, preferred_element_type=jnp.float32)
        * score_scale
    )
    query_sum = lax.psum(query_part.reshape(row_count, heads_per_group * HEAD_WIDTH), "seq")
    query_low = query_sum.astype(jnp.bfloat16)
    span_part = jnp.dot(query_low, w_query.T, preferred_element_type=jnp.float32)
    grad_span_input = lax.psum_scatter(span_part, "head", scatter_dimension=0, tiled=True).astype(
        jnp.bfloat16
    )
    saved_key_gradient = key_grads.astype(jnp.bfloat16)
    saved_value_gradient = value_grads.astype(jnp.bfloat16)
    key_weights, value_weights = (
        lax.all_to_all(key_projection_weight, "head", split_axis=0, concat_axis=1, tiled=True),
        lax.all_to_all(value_projection_weight, "head", split_axis=0, concat_axis=1, tiled=True),
    )
    key_all, value_all = (
        lax.all_gather(saved_key_gradient, "head", axis=1, tiled=True),
        lax.all_gather(saved_value_gradient, "head", axis=1, tiled=True),
    )
    total = jnp.zeros((block_size, key_weights.shape[0]), jnp.float32)
    for member in range(lax.axis_size("head")):
        first = member * HEAD_WIDTH
        both = jnp.concatenate(
            [key_all[:, first : first + HEAD_WIDTH], value_all[:, first : first + HEAD_WIDTH]],
            axis=1,
        )
        joined = jnp.concatenate(
            [
                key_weights[:, first : first + HEAD_WIDTH],
                value_weights[:, first : first + HEAD_WIDTH],
            ],
            axis=1,
        )
        partial_term = jnp.dot(both, joined.T, preferred_element_type=jnp.float32)
        rounded = lax.optimization_barrier(partial_term.astype(jnp.bfloat16))
        total = total + rounded.astype(jnp.float32)
    cached_input_gradient = total.astype(jnp.bfloat16)
    return (saved_key_gradient, saved_value_gradient, cached_input_gradient, grad_span_input)


def solution(mesh):
    in_specs = (
        P("seq", "head"),
        P("seq", "head"),
        P("seq", "head"),
        P("seq", "head"),
        P("seq"),
        P(),
        P("seq", "head"),
        P(None, "head"),
        P(None, "head"),
    )
    out_specs = (P("seq", "head"), P("seq", "head"), P("seq", "head"), P("head", "seq"))
    n, nh = mesh.shape["seq"], mesh.shape["head"]

    def device(queries, *rest):
        rows_own, width = queries.shape
        rows, heads = rows_own * n, width // HEAD_WIDTH
        fits = (
            n % 2 == 0
            and rows_own % 16 == 0
            and rows % 128 == 0
            and heads % n == 0
            and (heads // 2) % 8 == 0
            and (rows // nh) % 16 == 0
            and nh >= 3
            and rest[-1].shape[0] % (nh * n * 16) == 0
        )
        if not fits:
            return local(queries, *rest)
        return fused(n, nh, queries, *rest)

    return jax.shard_map(device, mesh=mesh, in_specs=in_specs, out_specs=out_specs, check_vma=False)
```

```python
import functools
import math

import jax
import jax.numpy as jnp
from jax import lax
from jax.experimental import pallas as pl
from jax.experimental.pallas import tpu as pltpu
from jax.sharding import PartitionSpec as P

HEAD_WIDTH = 128


LOWEST_SCORE = -1e30
PEAK_FLOOR = -1e29
MESH = pl.DeviceIdType.MESH
NT = (((1,), (1,)), ((), ()))


def dot_nt(a, b):
    return lax.dot_general(a, b, NT, preferred_element_type=jnp.float32)


def dot_nn(a, b):
    return jnp.dot(a, b, preferred_element_type=jnp.float32)


def kernel(
    n, nh,
    q_in, g_in, k_in, v_in, len_ref, span_ref, wq_in, kw_in, vw_in,
    dk_out, dv_out, cached_out, span_out,
    q_all, g_all, k_ref, v_ref, kt, len_all, bias, e_buf, dp_buf, st_all, fac, rterm,
    dv_acc, dk_acc, dq_send, dq_recv, dq_all, wq, w_all, dkv_all, acc,
    span_acc, span_send, span_recv,
    loc_sem, q_sem, g_sem, a_sem, len_sem, st_sem, rs_sem, w_sem, wf_sem, z_sem, h_sem,
):
    me, hd = lax.axis_index("seq"), lax.axis_index("head")
    nchip = n // 2
    core, chip = lax.rem(me, 2), me // 2
    sib = me + 1 - 2 * core
    rows_own = q_in.shape[0]
    rows = rows_own * n
    slots = k_in.shape[0]
    heads = q_in.shape[1] // HEAD_WIDTH
    hb = heads // n
    wid = hb * HEAD_WIDTH
    half_rows = heads // 2
    feats = kw_in.shape[0] // nh
    fh = feats // 2
    scale = HEAD_WIDTH ** (-0.5)

    def seq_peer(k):
        return lax.rem(me + k, n)

    def seq_from(k):
        return lax.rem(me + n - k, n)

    def head_peer(k):
        return lax.rem(hd + k, nh)

    def head_from(k):
        return lax.rem(hd + nh - k, nh)

    def remote(src, dst, ssem, rsem, s, h):
        return pltpu.make_async_remote_copy(
            src_ref=src, dst_ref=dst, send_sem=ssem, recv_sem=rsem,
            device_id=(s, h), device_id_type=MESH,
        )

    own_rows = pl.ds(pl.multiple_of(me * rows_own, rows_own), rows_own)
    own_feats = pl.ds(pl.multiple_of(hd * feats, feats), feats)
    local = [
        pltpu.make_async_copy(q_in, q_all.at[own_rows], loc_sem.at[0]),
        pltpu.make_async_copy(g_in, g_all.at[own_rows], loc_sem.at[1]),
        pltpu.make_async_copy(wq_in, wq, loc_sem.at[2]),
        pltpu.make_async_copy(kw_in.at[own_feats], w_all.at[2 * hd], loc_sem.at[3]),
        pltpu.make_async_copy(vw_in.at[own_feats], w_all.at[2 * hd + 1], loc_sem.at[4]),
        pltpu.make_async_copy(k_in, k_ref, loc_sem.at[5]),
        pltpu.make_async_copy(v_in, v_ref, loc_sem.at[6]),
    ]
    for i in (0, 1, 5, 6):
        local[i].start()
    len_all[me] = jnp.full((8, 128), len_ref[0], jnp.int32)

    barrier = pltpu.get_barrier_semaphore()
    for k in range(1, n):
        pl.semaphore_signal(barrier, inc=1, device_id=(seq_peer(k), hd), device_id_type=MESH)
    for k in range(1, nh):
        pl.semaphore_signal(barrier, inc=1, device_id=(me, head_peer(k)), device_id_type=MESH)
    pl.semaphore_wait(barrier, n - 1 + nh - 1)

    def chip_peer(k):
        return 2 * lax.rem(chip + k, nchip) + core

    def chip_from(k):
        return 2 * lax.rem(chip + nchip - k, nchip) + core

    def gather_copy(k, src, slot, sem):
        to = sib if k == 0 else chip_peer(k)
        return remote(src, slot(me), sem.at[0, k], sem.at[1, k], to, hd)

    def forward_copy(k, slot, sem):
        block = slot(chip_from(k))
        return remote(block, block, sem.at[2, k], sem.at[3, k], sib, hd)

    def gather_start(src, slot, sem):
        for k in range(nchip):
            gather_copy(k, src, slot, sem).start()

    def gather_relay(src, slot, sem):
        for k in range(1, nchip):
            gather_copy(k, src, slot, sem).wait_recv()
            forward_copy(k, slot, sem).start()

    def gather_finish(src, slot, sem):
        gather_copy(0, src, slot, sem).wait_recv()
        for k in range(1, nchip):
            forward_copy(k, slot, sem).wait_recv()

    def gather_drain(src, slot, sem):
        for k in range(nchip):
            gather_copy(k, src, slot, sem).wait_send()
        for k in range(1, nchip):
            forward_copy(k, slot, sem).wait_send()

    def row_slot(buf):
        return lambda s: buf.at[pl.ds(pl.multiple_of(s * rows_own, rows_own), rows_own)]

    q_args = (q_in, row_slot(q_all), q_sem)
    g_args = (g_in, row_slot(g_all), g_sem)
    a_args = (dq_all.at[me], lambda s: dq_all.at[s], a_sem)

    def len_copy(k):
        return remote(
            len_all.at[me], len_all.at[me], len_sem.at[0, k], len_sem.at[1, k], seq_peer(k), hd
        )


    core_feats = pl.ds(pl.multiple_of(core * fh, fh), fh)

    def weight_copy(k, which):
        to = head_peer(k)
        src = (kw_in, vw_in)[which].at[pl.ds(pl.multiple_of(to * feats + core * fh, fh), fh)]
        return remote(
            src, w_all.at[2 * hd + which, core_feats],
            w_sem.at[0, which, k], w_sem.at[1, which, k], me, to,
        )

    def weight_forward(k):
        block = w_all.at[pl.ds(2 * head_from(k), 2), core_feats]
        return remote(block, block, wf_sem.at[0, k], wf_sem.at[1, k], sib, hd)

    for k in range(1, nh):
        for which in range(2):
            weight_copy(k, which).start()
    gather_start(*q_args)
    for k in range(1, n):
        len_copy(k).start()
    gather_start(*g_args)

    for i in (3, 4, 2):
        local[i].start()

    local[5].wait()
    kt[...] = k_ref[...].T
    local[6].wait()
    gather_relay(*q_args)
    gather_relay(*g_args)

    for k in range(1, n):
        len_copy(k).wait_recv()
    offset = jnp.zeros((8, 128), jnp.int32)
    for t in range(n):
        offset = offset + len_all[t] * (t < me).astype(jnp.int32)
    within = lax.broadcasted_iota(jnp.int32, (slots, rows), 0)
    qpos = span_ref[0] * rows + lax.broadcasted_iota(jnp.int32, (slots, rows), 1)
    visible = (within < len_ref[0]) & (offset[0:1, 0:1] + within <= qpos)
    bias[...] = jnp.where(visible, 0.0, LOWEST_SCORE)

    local[0].wait()
    local[1].wait()
    gather_finish(*q_args)
    gather_finish(*g_args)

    def pair(buf, j):
        block = buf[:, pl.ds(pl.multiple_of(j * wid, wid), wid)]
        return jnp.concatenate(
            [block[:, i * HEAD_WIDTH : (i + 1) * HEAD_WIDTH] for i in range(hb)], axis=0
        )

    def st_copy(half, k):
        return remote(
            st_all.at[half, me], st_all.at[half, me],
            st_sem.at[0, half, k], st_sem.at[1, half, k], seq_peer(k), hd,
        )

    for half in range(2):

        def first(i, carry, half=half):
            place = lax.rem(chip + 1 + i, nchip)
            j = 2 * place + half
            s = dot_nt(k_ref[...], pair(q_all, j)) * (scale * math.log2(math.e))
            s = s + jnp.concatenate([bias[...]] * hb, axis=1)
            m = jnp.maximum(jnp.max(s, axis=0, keepdims=True), PEAK_FLOOR)
            e = jnp.exp2(s - m)
            dp = dot_nt(v_ref[...], pair(g_all, j))
            e_buf[j] = e
            dp_buf[j] = dp
            stats = (m, jnp.sum(e, axis=0, keepdims=True), jnp.sum(e * dp, axis=0, keepdims=True))
            for at, stat in enumerate(stats):
                for h in range(hb):
                    st_all[half, me, pl.ds(at * half_rows + place * hb + h, 1), :] = stat[
                        :, h * rows : (h + 1) * rows
                    ]
            return carry

        lax.fori_loop(0, nchip, first, 0)
        for k in range(1, n):
            st_copy(half, k).start()

    def rs_copy(k, to):
        return remote(dq_send.at[to], dq_recv.at[me], rs_sem.at[0, k], rs_sem.at[1, k], to, hd)

    dv_acc[...] = jnp.zeros_like(dv_acc)
    dk_acc[...] = jnp.zeros_like(dk_acc)
    for half in range(2):
        for k in range(1, n):
            st_copy(half, k).wait_recv()
        part = lambda t, at: st_all[half, t, at * half_rows : (at + 1) * half_rows, :]
        peak = part(0, 0)
        for t in range(1, n):
            peak = jnp.maximum(peak, part(t, 0))
        total = jnp.zeros_like(peak)
        numer = jnp.zeros_like(peak)
        for t in range(n):
            f = jnp.exp2(part(t, 0) - peak)
            total = total + part(t, 1) * f
            numer = numer + part(t, 2) * f
        fac[half] = jnp.exp2(part(me, 0) - peak) / total
        rterm[half] = numer / total

        def second(i, carry, half=half):
            place = lax.rem(chip + 1 + i, nchip)
            j = 2 * place + half
            line = lambda ref: jnp.concatenate(
                [ref[half, pl.ds(place * hb + h, 1), :] for h in range(hb)], axis=1
            )
            p = e_buf[j] * line(fac)
            ds = (p * (dp_buf[j] - line(rterm))).astype(jnp.bfloat16)
            dv_acc[...] += dot_nn(p.astype(jnp.bfloat16), pair(g_all, j))
            dq_send[j] = (dot_nn(kt[...], ds) * scale).astype(jnp.bfloat16)

            @pl.when(j != me)
            def _():
                rs_copy(lax.rem(j + n - me, n), j).start()

            dk_acc[...] += dot_nn(ds, pair(q_all, j))
            return carry

        lax.fori_loop(0, nchip, second, 0)

    dk_low = (dk_acc[...] * scale).astype(jnp.bfloat16)
    dv_low = dv_acc[...].astype(jnp.bfloat16)
    dkv_all[2 * hd] = dk_low
    dkv_all[2 * hd + 1] = dv_low

    def z_send(way, d, w):
        src = hd - (d - 1) if way == 0 else hd + (d - 1)
        to = hd + 1 if way == 0 else hd - 1
        block = dkv_all.at[2 * src + w]
        ok = (src >= 0) & (src < nh) & (to >= 0) & (to < nh)
        return ok, remote(block, block, z_sem.at[0, way, d, w], z_sem.at[1, way, d, w], me, to)

    def z_recv(way, d, w):
        src = hd - d if way == 0 else hd + d
        block = dkv_all.at[2 * src + w]
        ok = (src >= 0) & (src < nh)
        return ok, src, remote(
            block, block, z_sem.at[0, way, d, w], z_sem.at[1, way, d, w], me, head_peer(1)
        )

    def z_start(d, w):
        for way in range(2):
            ok, c = z_send(way, d, w)
            pl.when(ok)(c.start)

    def z_hop(d, w):
        for way in range(2):
            ok, _, c = z_recv(way, d - 1, w)
            pl.when(ok)(c.wait_recv)
            ok, c = z_send(way, d, w)
            pl.when(ok)(c.start)

    z_start(1, 1)
    z_start(1, 0)
    dk_out[...] = dk_low
    dv_out[...] = dv_low

    total = dq_send[me].astype(jnp.float32)
    for k in range(1, n):
        rs_copy(k, seq_peer(k)).wait_recv()
        total = total + dq_recv[seq_from(k)].astype(jnp.float32)
    for h in range(hb):
        dq_all[me, :, h * HEAD_WIDTH : (h + 1) * HEAD_WIDTH] = (
            total[:, h * rows : (h + 1) * rows].T.astype(jnp.bfloat16)
        )
    gather_start(*a_args)

    z_hop(2, 1)
    z_hop(2, 0)
    for k in range(1, nh):
        weight_copy(k, 0).wait_recv()
        weight_copy(k, 1).wait_recv()
        weight_forward(k).start()

    local[3].wait()
    local[4].wait()
    tile = min(256, feats)

    def term(g, start):
        lhs = jnp.concatenate([dkv_all[2 * g], dkv_all[2 * g + 1]], axis=1)

        def one(i, carry):
            at = pl.ds(pl.multiple_of(i * tile, tile), tile)
            rhs = jnp.concatenate([w_all[2 * g, at, :], w_all[2 * g + 1, at, :]], axis=1)
            x = dot_nt(lhs, rhs)
            acc[:, at] = x if start else x + acc[:, at]
            return carry

        lax.fori_loop(0, feats // tile, one, 0)

    local[2].wait()
    gather_relay(*a_args)
    term(hd, True)

    def span_add(s):
        cols = pl.ds(pl.multiple_of(s * wid, wid), wid)
        return dot_nt(dq_all[s], wq[:, cols])

    span_acc[...] = span_add(me)
    for k in range(1, nchip):
        span_acc[...] += span_add(chip_from(k))
    gather_finish(*a_args)

    def other(i, carry):
        span_acc[...] += span_add(2 * i + 1 - core)
        return carry

    lax.fori_loop(0, nchip, other, 0)

    span_rows = rows // nh
    span_send[...] = span_acc[...].astype(jnp.bfloat16).reshape(span_send.shape)

    def h_copy(k):
        to = head_peer(k)
        return remote(span_send.at[to], span_recv.at[hd], h_sem.at[0, k], h_sem.at[1, k], me, to)

    for k in range(1, nh):
        h_copy(k).start()

    for d in range(3, nh):
        z_hop(d, 1)
        z_hop(d, 0)
    for k in range(1, nh):
        weight_forward(k).wait_recv()
    for d in range(1, nh):
        for way in range(2):
            ok, src, last_v = z_recv(way, d, 1)
            last_k = z_recv(way, d, 0)[2]

            @pl.when(ok)
            def _(src=src, last_v=last_v, last_k=last_k, d=d):
                if d == nh - 1:
                    last_v.wait_recv()
                    last_k.wait_recv()
                term(src, False)

    cached_out[...] = acc[...].astype(cached_out.dtype)

    own_span = pl.ds(pl.multiple_of(hd * span_rows, span_rows), span_rows)
    total = span_acc[own_span, :]
    for k in range(1, nh):
        h_copy(k).wait_recv()
        total = total + span_recv[head_from(k)].astype(jnp.float32)
    span_out[...] = total.astype(span_out.dtype)

    gather_drain(*q_args)
    gather_drain(*g_args)
    gather_drain(*a_args)
    for k in range(1, n):
        len_copy(k).wait_send()
        rs_copy(k, seq_peer(k)).wait_send()
        for half in range(2):
            st_copy(half, k).wait_send()
    for k in range(1, nh):
        weight_copy(k, 0).wait_send()
        weight_copy(k, 1).wait_send()
        weight_forward(k).wait_send()
        for way in range(2):
            for w in range(2):
                ok, c = z_send(way, k, w)
                pl.when(ok)(c.wait_send)
        h_copy(k).wait_send()


def fused(
    n, nh, queries, grad_output, key_cache, saved_value_rows, lengths, span_index,
    w_query, key_projection_weight, value_projection_weight,
):
    rows_own, width = queries.shape
    rows, heads = rows_own * n, width // HEAD_WIDTH
    wid = width // n
    slots = key_cache.shape[0]
    feats = key_projection_weight.shape[0] // nh
    out_feats = w_query.shape[0]
    nchip = n // 2
    bf, f32 = jnp.bfloat16, jnp.float32
    vmem = pl.BlockSpec(memory_space=pltpu.VMEM)
    smem = pl.BlockSpec(memory_space=pltpu.SMEM)
    hbm = pl.BlockSpec(memory_space=pltpu.HBM)
    dma = pltpu.SemaphoreType.DMA
    V = pltpu.VMEM
    hq = wid // HEAD_WIDTH * rows
    results = pl.pallas_call(
        functools.partial(kernel, n, nh),
        out_shape=(
            jax.ShapeDtypeStruct((slots, HEAD_WIDTH), bf),
            jax.ShapeDtypeStruct((slots, HEAD_WIDTH), bf),
            jax.ShapeDtypeStruct((slots, feats), bf),
            jax.ShapeDtypeStruct((rows // nh, out_feats), bf),
        ),
        in_specs=[hbm, hbm, hbm, hbm, smem, smem, hbm, hbm, hbm],
        out_specs=(vmem, vmem, vmem, vmem),
        scratch_shapes=[
            V((rows, width), bf),
            V((rows, width), bf),
            V((slots, HEAD_WIDTH), bf),
            V((slots, HEAD_WIDTH), bf),
            V((HEAD_WIDTH, slots), bf),
            V((n, 8, 128), jnp.int32),
            V((slots, rows), f32),
            V((n, slots, hq), f32),
            V((n, slots, hq), f32),
            V((2, n, 3 * heads // 2, rows), f32),
            V((2, heads // 2, rows), f32),
            V((2, heads // 2, rows), f32),
            V((slots, HEAD_WIDTH), f32),
            V((slots, HEAD_WIDTH), f32),
            V((n, HEAD_WIDTH, hq), bf),
            V((n, HEAD_WIDTH, hq), bf),
            V((n, rows, wid), bf),
            V((out_feats, width), bf),
            V((2 * nh, feats, HEAD_WIDTH), bf),
            V((2 * nh, slots, HEAD_WIDTH), bf),
            V((slots, feats), f32),
            V((rows, out_feats), f32),
            V((nh, rows // nh, out_feats), bf),
            V((nh, rows // nh, out_feats), bf),
            dma((7,)),
            dma((4, nchip)),
            dma((4, nchip)),
            dma((4, nchip)),
            dma((2, n)),
            dma((2, 2, n)),
            dma((2, n)),
            dma((2, 2, nh)),
            dma((2, nh)),
            dma((2, 2, nh, 2)),
            dma((2, nh)),
        ],
        compiler_params=pltpu.CompilerParams(
            collective_id=0, has_side_effects=True, vmem_limit_bytes=63 * 1024 * 1024
        ),
    )(
        queries, grad_output, key_cache, saved_value_rows, lengths, span_index,
        w_query, key_projection_weight, value_projection_weight,
    )
    count = len(results)
    return pl.pallas_call(
        functools.partial(write_out, count),
        out_shape=tuple(jax.ShapeDtypeStruct(r.shape, r.dtype) for r in results),
        in_specs=[vmem] * count,
        out_specs=(hbm,) * count,
        scratch_shapes=[dma((count,))],
    )(*results)


def write_out(count, *refs):
    sem = refs[-1]
    copies = [
        pltpu.make_async_copy(refs[i], refs[count + i], sem.at[i]) for i in range(count)
    ]
    for c in copies:
        c.start()
    for c in copies:
        c.wait()


def prefix(part, axis, combine, identity):
    place = lax.axis_index(axis)
    gathered = lax.all_gather(part, axis)
    state = jnp.zeros_like(part) + jnp.asarray(identity, part.dtype)

    def one(lap, state):
        return combine(state, lax.dynamic_index_in_dim(gathered, lap, 0, False))

    return lax.fori_loop(0, place, one, state)


def merged(part, axis, combine):
    gathered = jax.tree.map(lambda a: lax.all_gather(a, axis), part)

    def take(source):
        return jax.tree.map(lambda a: lax.dynamic_index_in_dim(a, source, 0, False), gathered)

    return lax.fori_loop(
        1, lax.axis_size(axis), lambda source, state: combine(state, take(source)), take(0)
    )


def add_counts(earlier, later):
    return earlier + later


def pair_merge(first, second):
    joined_peak = jnp.maximum(first[0], second[0])
    first_factor = jnp.exp(first[0] - joined_peak)
    second_factor = jnp.exp(second[0] - joined_peak)
    return (joined_peak, first[1] * first_factor + second[1] * second_factor)


def local(
    queries,
    grad_output,
    key_cache,
    saved_value_rows,
    lengths,
    span_index,
    w_query,
    key_projection_weight,
    value_projection_weight,
):
    score_scale = HEAD_WIDTH ** (-0.5)
    offset = prefix(lengths, "seq", add_counts, jnp.zeros((1,), jnp.int32))
    query_all, grad_all = (
        lax.all_gather(queries, "seq", axis=0, tiled=True),
        lax.all_gather(grad_output, "seq", axis=0, tiled=True),
    )
    row_count = query_all.shape[0]
    block_size = key_cache.shape[0]
    heads_per_group = query_all.shape[1] // HEAD_WIDTH
    within = jnp.arange(block_size, dtype=jnp.int32)
    query_positions = span_index[0] * row_count + jnp.arange(row_count, dtype=jnp.int32)
    visible = (within < lengths[0])[None, :] & (
        (offset[0] + within)[None, :] <= query_positions[:, None]
    )
    visible = visible[None, :, :]
    query_heads = query_all.reshape(row_count, heads_per_group, HEAD_WIDTH)
    grad_heads = grad_all.reshape(row_count, heads_per_group, HEAD_WIDTH)
    scores = (
        jnp.einsum("ihd,pd->hip", query_heads, key_cache, preferred_element_type=jnp.float32)
        * score_scale
    )
    weight_grads = jnp.einsum(
        "ihd,pd->hip", grad_heads, saved_value_rows, preferred_element_type=jnp.float32
    )
    local_peak = jnp.max(jnp.where(visible, scores, LOWEST_SCORE), axis=2)
    local_exp = jnp.exp(jnp.where(visible, scores - local_peak[:, :, None], LOWEST_SCORE))
    local_total = jnp.sum(local_exp, axis=2)
    row_peak, row_total = merged((local_peak, local_total), "seq", pair_merge)
    weights = (
        jnp.exp(jnp.where(visible, scores - row_peak[:, :, None], LOWEST_SCORE))
        / row_total[:, :, None]
    )
    row_terms = lax.psum(jnp.sum(weights * weight_grads, axis=2), "seq")
    score_grads = weights * (weight_grads - row_terms[:, :, None])
    weights_low = weights.astype(jnp.bfloat16)
    score_low = score_grads.astype(jnp.bfloat16)
    value_grads = jnp.einsum(
        "hip,ihd->pd", weights_low, grad_heads, preferred_element_type=jnp.float32
    )
    key_grads = (
        jnp.einsum("hip,ihd->pd", score_low, query_heads, preferred_element_type=jnp.float32)
        * score_scale
    )
    query_part = (
        jnp.einsum("hip,pd->ihd", score_low, key_cache, preferred_element_type=jnp.float32)
        * score_scale
    )
    query_sum = lax.psum(query_part.reshape(row_count, heads_per_group * HEAD_WIDTH), "seq")
    query_low = query_sum.astype(jnp.bfloat16)
    span_part = jnp.dot(query_low, w_query.T, preferred_element_type=jnp.float32)
    grad_span_input = lax.psum_scatter(span_part, "head", scatter_dimension=0, tiled=True).astype(
        jnp.bfloat16
    )
    saved_key_gradient = key_grads.astype(jnp.bfloat16)
    saved_value_gradient = value_grads.astype(jnp.bfloat16)
    key_weights, value_weights = (
        lax.all_to_all(key_projection_weight, "head", split_axis=0, concat_axis=1, tiled=True),
        lax.all_to_all(value_projection_weight, "head", split_axis=0, concat_axis=1, tiled=True),
    )
    key_all, value_all = (
        lax.all_gather(saved_key_gradient, "head", axis=1, tiled=True),
        lax.all_gather(saved_value_gradient, "head", axis=1, tiled=True),
    )
    total = jnp.zeros((block_size, key_weights.shape[0]), jnp.float32)
    for member in range(lax.axis_size("head")):
        first = member * HEAD_WIDTH
        both = jnp.concatenate(
            [key_all[:, first : first + HEAD_WIDTH], value_all[:, first : first + HEAD_WIDTH]],
            axis=1,
        )
        joined = jnp.concatenate(
            [
                key_weights[:, first : first + HEAD_WIDTH],
                value_weights[:, first : first + HEAD_WIDTH],
            ],
            axis=1,
        )
        partial_term = jnp.dot(both, joined.T, preferred_element_type=jnp.float32)
        rounded = lax.optimization_barrier(partial_term.astype(jnp.bfloat16))
        total = total + rounded.astype(jnp.float32)
    cached_input_gradient = total.astype(jnp.bfloat16)
    return (saved_key_gradient, saved_value_gradient, cached_input_gradient, grad_span_input)


def solution(mesh):
    in_specs = (
        P("seq", "head"),
        P("seq", "head"),
        P("seq", "head"),
        P("seq", "head"),
        P("seq"),
        P(),
        P("seq", "head"),
        P(None, "head"),
        P(None, "head"),
    )
    out_specs = (P("seq", "head"), P("seq", "head"), P("seq", "head"), P("head", "seq"))
    n, nh = mesh.shape["seq"], mesh.shape["head"]

    def device(queries, *rest):
        rows_own, width = queries.shape
        rows, heads = rows_own * n, width // HEAD_WIDTH
        fits = (
            n % 2 == 0
            and rows_own % 16 == 0
            and rows % 128 == 0
            and heads % n == 0
            and (heads // 2) % 8 == 0
            and (rows // nh) % 16 == 0
            and nh >= 3
            and rest[-1].shape[0] % (nh * n * 16) == 0
        )
        if not fits:
            return local(queries, *rest)
        return fused(n, nh, queries, *rest)

    return jax.shard_map(device, mesh=mesh, in_specs=in_specs, out_specs=out_specs, check_vma=False)
```
